768 devices in a mesh: prod: 12 (over z), store: 64 (over y, x, core).
Axes of the slice: x: 4, y: 8, z: 12, core: 2. Of those that a mesh axis runs over, the one named last changes fastest.
Arguments:
- tiles: bfloat16 [49152, 64, 512], P(('prod', 'store')), may hold values from -6 to 6
- tile_blocks: int32 [768, 64, 2], P(('prod', 'store')), may hold values from 0 to 63, as said below
- counts: int32 [768], P(('prod', 'store')), may hold values from 16 to 64, as said below
- fetch_list: int32 [768, 64, 1], P(('prod', 'store')), may hold values from 0 to 511, as said below
- store_factor: bfloat16 [32768, 128], P('store'), may hold values from -0.29882812 to 0.29882812
- day_factor: bfloat16 [8, 128], replicated, may hold values from -0.08984375 to 0.08984375
Outputs:
- product_factor: float32 [12288, 128], P(('prod', 'store'))
The draws below stay inside these ranges and needn't reach their ends.
Inputs may be any that keep to these rules, and one draw needn't show every extreme that they name: `tile_blocks`: product block within the group (16) in column 0; in column 1 each device's slots name 64 different entries of its store list, a permutation. `counts`: one device in every draw has all 64 slots live. `fetch_list`: row o of a device's list holds 1 different store blocks owned by store index o, o * 8 to (o + 1) * 8 - 1.
All inputs are finite; a program needn't handle non-finite values.
Results may differ from the reference program's by a relative error of at most 0.007.
Values may be sent and summed in bfloat16 or wider, within the bound.
A program may use at most 32 MiB of HBM per device.

```python
import jax
import jax.numpy as jnp
from jax import lax

RANK = 128
TP = 64
TS = 64
DAYS = 8
PB_DEV = 16
SB_DEV = 8
TILE_DEV = 64
CAP = 1
PRODUCTS = 12288
STORE_BLOCKS = 512
STORES = 32768
SLOTS = 64
N_PROD = 12
N_STORE = 64


def draw_tile_blocks(key, part):
    key = jax.random.fold_in(key, 11)
    first, second = jax.random.split(key)
    total = N_PROD * N_STORE
    block_col = jax.random.randint(first, (total, TILE_DEV, 1), 0, PB_DEV, dtype=jnp.int32)
    device_keys = jax.random.split(second, total)
    orders = jax.vmap(lambda k: jax.random.permutation(k, SLOTS))(device_keys).astype(jnp.int32)
    return jnp.concatenate([block_col, orders[:, :TILE_DEV, None]], axis=2)


def draw_fetch_list(key, part):
    key = jax.random.fold_in(key, 12)
    total = N_PROD * N_STORE * N_STORE
    owner_keys = jax.random.split(key, total)
    picks = jax.vmap(lambda k: jax.random.permutation(k, SB_DEV)[:CAP])(owner_keys).astype(jnp.int32)
    picks = picks.reshape(N_PROD * N_STORE, N_STORE, CAP)
    owner = (jnp.arange(N_STORE, dtype=jnp.int32) * SB_DEV)[None, :, None]
    return (owner + picks).astype(jnp.int32)


def draw_counts(key, part):
    key = jax.random.fold_in(key, 13)
    first, second, third = jax.random.split(key, 3)
    total = N_PROD * N_STORE
    spread = 3 * TILE_DEV // 4
    left = jax.random.randint(first, (total,), 0, spread + 1, dtype=jnp.int32)
    right = jax.random.randint(second, (total,), 0, spread + 1, dtype=jnp.int32)
    base = TILE_DEV // 4 + left * right // (spread + 1)
    chosen = jax.random.randint(third, (), 0, total, dtype=jnp.int32)
    return jnp.where(jnp.arange(total, dtype=jnp.int32) == chosen, TILE_DEV, base).astype(jnp.int32)


def shard_levels(own_key, shape, cuts, least, high):
    loudness = 1.0
    for dim, parts in cuts:
        draws = jax.random.uniform(jax.random.fold_in(jax.random.fold_in(own_key, 6), dim), (parts,), jnp.float32, least / len(cuts), high / len(cuts))
        loudness = loudness * jnp.repeat(jnp.exp(draws), shape[dim] // parts).reshape((-1,) + (1,) * (len(shape) - 1 - dim))
    return loudness


def noise(own_key, dims, width, bound, cuts=(), held_as=jnp.bfloat16):
    entries = width * jax.random.normal(own_key, dims, jnp.float32)
    if cuts:
        entries = entries * shard_levels(own_key, dims, cuts, -0.22, 0.18)
    return jnp.clip(entries, -bound, bound).astype(held_as)


def setup_inputs(seed: int = 0) -> dict:
    seeds = jax.random.split(jax.random.key(seed), 7)
    tiles = noise(seeds[0], (N_PROD * N_STORE * TILE_DEV, TP, TS * DAYS), 1.0, 6.0, ((0, 768),))
    tile_blocks = draw_tile_blocks(jax.random.fold_in(seeds[6], 71), 0)
    counts = draw_counts(jax.random.fold_in(seeds[6], 71), 0)
    fetch_list = draw_fetch_list(jax.random.fold_in(seeds[6], 71), 0)
    store_factor = noise(seeds[4], (STORES, RANK), 0.05, 0.29882812, ((0, 64),))
    day_factor = noise(seeds[5], (DAYS, RANK), 0.015, 0.08984375)
    return dict(tiles=tiles, tile_blocks=tile_blocks, counts=counts, fetch_list=fetch_list, store_factor=store_factor, day_factor=day_factor)


def device_part(tile_vals, block_ids, count, fetch_dev, factor_blocks, day_factor):
    table = factor_blocks[fetch_dev.reshape(-1)]
    rows = table[block_ids[:, 1]]
    kron = rows.astype(jnp.float32)[:, :, None, :] * day_factor.astype(jnp.float32)[None, None, :, :]
    kron = kron.reshape(TILE_DEV, TS * DAYS, RANK).astype(jnp.bfloat16)
    contrib = jnp.einsum('tij,tjr->tir', tile_vals.astype(jnp.float32), kron.astype(jnp.float32), precision=lax.Precision.HIGHEST)
    live = (jnp.arange(TILE_DEV, dtype=jnp.int32) < count).astype(jnp.float32)
    onehot = (block_ids[:, 0][:, None] == jnp.arange(PB_DEV, dtype=jnp.int32)[None, :]).astype(jnp.float32) * live[:, None]
    return jnp.einsum('tp,tir->pir', onehot, contrib, precision=lax.Precision.HIGHEST).reshape(PB_DEV * TP, RANK)

def reference(tiles, tile_blocks, counts, fetch_list, store_factor, day_factor):
    tiles_dev = tiles.reshape(N_PROD * N_STORE, TILE_DEV, TP, TS * DAYS)
    factor_blocks = store_factor.reshape(STORE_BLOCKS, TS, RANK)

    def step(total, device):
        part = device_part(tiles_dev[device], tile_blocks[device], counts[device], fetch_list[device], factor_blocks, day_factor)
        return (total.at[device // N_STORE].add(part), None)
    total = jnp.zeros((N_PROD, PB_DEV * TP, RANK), jnp.float32)
    total, unused = lax.scan(step, total, jnp.arange(N_PROD * N_STORE, dtype=jnp.int32))
    mttkrp = total.reshape(PRODUCTS, RANK)
    gram_store = jnp.dot(store_factor.T.astype(jnp.float32), store_factor.astype(jnp.float32), preferred_element_type=jnp.float32)
    gram_day = jnp.dot(day_factor.T.astype(jnp.float32), day_factor.astype(jnp.float32), preferred_element_type=jnp.float32)
    gram = gram_store * gram_day
    lower = jnp.linalg.cholesky(gram)
    return jax.scipy.linalg.cho_solve((lower, True), mttkrp.T).T
```

```python
import jax
import jax.numpy as jnp
from jax import lax
from jax.experimental import pallas as pl
from jax.experimental.pallas import tpu as pltpu
from jax.sharding import PartitionSpec as P

PB = 16
SB = 8
TS = 64
RANK = 128
DAYS = 8
X = 8
Y = 8
HIGHEST = lax.Precision.HIGHEST
F32 = jnp.float32


def rows_sum(x):
    return jnp.sum(x, axis=0, keepdims=True)


def cols_sum(x):
    return jnp.sum(x, axis=1, keepdims=True)


def plan(blocks, count):
    slots = blocks.shape[1]
    sub = lax.broadcasted_iota(jnp.int32, (slots, slots), 0)
    lane = lax.broadcasted_iota(jnp.int32, (slots, slots), 1)
    lane_row = lax.broadcasted_iota(jnp.int32, (1, slots), 1)
    p_row, perm_row = blocks[0:1, :], blocks[1:2, :]
    key_row = jnp.where(lane_row < count, p_row * slots, PB * slots * 4) + perm_row
    eye = sub == lane
    perm_col = cols_sum(jnp.where(eye, perm_row, 0))
    key_col = cols_sum(jnp.where(eye, key_row, 0))
    rank_col = cols_sum(jnp.where(key_row < key_col, 1, 0))
    tile_of = rows_sum(jnp.where(perm_col == lane, sub, 0))
    order = rows_sum(jnp.where(rank_col == lane, perm_col, 0))
    block_at = rows_sum(jnp.where(rank_col == lane, key_col // slots, 0))
    block_before = rows_sum(jnp.where(rank_col + 1 == lane, key_col // slots, 0))
    same = jnp.where((block_at == block_before) & (lane_row > 0), 1, 0)
    ends = rows_sum(jnp.where(key_col < (lane + 1) * slots, 1, 0))
    begins = rows_sum(jnp.where(key_col < lane * slots, 1, 0))
    return tile_of, order, same, ends, begins


def kernel(
    tiles_hbm, blocks_ref, count_ref, fetch_ref, store_hbm, day_ref, out_ref,
    tiles, own, right1, right2, right3, left1, left2, left3, far,
    table, stage, contribs, sums,
    plan_v, plan_s, my_list, lists_v, lists_s,
    gram_part, gram_y, gram_mine, gram_x, gram_sum, gram, inverse,
    send_x, recv_x, send_y, recv_y,
    local_sem, ring_s, ring_r, list_s, list_r, block_s, block_r,
    gy_s, gy_r, gx_s, gx_r, gg_s, gg_r, rx_s, rx_r, ry_s, ry_r,
):
    me = lax.axis_index("store")
    y, q = me // X, me % X

    def x_peer(d):
        return y * X + (q + d) % X

    def y_peer(e):
        return (y + e) % Y * X + q

    def to(src, dst, send, recv, target):
        return pltpu.make_async_remote_copy(
            src_ref=src, dst_ref=dst, send_sem=send, recv_sem=recv,
            device_id={"store": target}, device_id_type=pl.DeviceIdType.MESH,
        )

    def each(first, last, body):
        def step(i, carry):
            body(i)
            return carry
        lax.fori_loop(first, last, step, 0)

    load_own = pltpu.make_async_copy(store_hbm, own, local_sem.at[0])
    load_own.start()
    load_tiles = pltpu.make_async_copy(tiles_hbm, tiles, local_sem.at[1])
    load_tiles.start()
    barrier = pltpu.get_barrier_semaphore()
    each(1, X, lambda d: pl.semaphore_signal(
        barrier, inc=1, device_id={"store": x_peer(d)}, device_id_type=pl.DeviceIdType.MESH))
    each(1, Y, lambda e: pl.semaphore_signal(
        barrier, inc=1, device_id={"store": y_peer(e)}, device_id_type=pl.DeviceIdType.MESH))

    for row, value in enumerate(plan(blocks_ref[...], count_ref[0])):
        plan_v[row : row + 1, 0:64] = value
    my_list[0:1, 0:64] = fetch_ref[...]
    load_plan = pltpu.make_async_copy(plan_v, plan_s, local_sem.at[2])
    load_plan.start()
    load_own.wait()
    gram_part[...] = lax.dot_general(
        own[...].reshape(SB * TS, RANK), own[...].reshape(SB * TS, RANK),
        (((0,), (0,)), ((), ())), preferred_element_type=F32,
    )
    load_plan.wait()
    pl.semaphore_wait(barrier, X + Y - 2)

    rights, lefts = [right1, right2, right3, far], [left1, left2, left3, far]
    half = SB // 2

    def ring(direction, step, part):
        bufs = rights if direction == 0 else lefts
        src = own if step == 0 else bufs[step - 1]
        cut = pl.ds(part * half, half)
        return to(
            src.at[cut], bufs[step].at[cut],
            ring_s.at[direction, step, part], ring_r.at[direction, step, part],
            y_peer(1 if direction == 0 else Y - 1),
        )

    for part in range(2):
        ring(0, 0, part).start()
        ring(1, 0, part).start()

    def list_copy(d):
        return to(my_list, lists_v.at[d], list_s.at[d], list_r.at[d], x_peer(d))

    each(1, X, lambda d: list_copy(d).start())

    def gram_y_copy(e):
        return to(
            gram_part.at[pl.ds((y + e) % Y * 16, 16)], gram_y.at[y],
            gy_s.at[e], gy_r.at[e], y_peer(e),
        )

    each(1, Y, lambda e: gram_y_copy(e).start())
    gram_y[y] = gram_part[pl.ds(y * 16, 16), :]

    lists_v[0] = my_list[...]
    each(1, X, lambda d: list_copy(d).wait_recv())
    load_lists = pltpu.make_async_copy(lists_v, lists_s, local_sem.at[3])
    load_lists.start()
    load_lists.wait()

    def block_copy(k, d):
        return to(stage.at[k, d], table.at[k, d], block_s.at[k, d], block_r.at[k, d], x_peer(d))

    def owner(k, d):
        shift = (0, Y - 1, 1, Y - 2, 2, Y - 3, 3, 4)[k]
        return (y + shift) % Y * X + (q + X - d) % X

    def serve(k, buf):
        mine = owner(k, 0)
        table[k, 0] = buf[lists_s[0, 0, mine] & (SB - 1)]

        def one(d):
            stage[k, d] = buf[lists_s[X - d, 0, mine] & (SB - 1)]
            block_copy(k, d).start()

        each(1, X, one)

    day = day_ref[...].astype(F32)

    def contribute(k):
        def one(d):
            entry = owner(k, d)
            rows = table[k, d].astype(F32)
            kron = (rows[:, None, :] * day[None, :, :]).reshape(TS * DAYS, RANK).astype(jnp.bfloat16)
            contribs[entry] = jnp.dot(
                tiles[plan_s[0, entry] & 63], kron, preferred_element_type=F32
            )

        each(1, X, lambda d: block_copy(k, d).wait_recv())
        each(0, X, one)

    def forward(step):
        for part in range(2):
            for direction in range(2):
                ring(direction, step - 1, part).wait_recv()
                if step < 3 or part == direction:
                    ring(direction, step, part).start()

    lane8 = lax.broadcasted_iota(jnp.int32, (8, RANK), 1)
    sub8 = lax.broadcasted_iota(jnp.int32, (8, RANK), 0)
    lane_all = lax.broadcasted_iota(jnp.int32, (RANK, RANK), 1)

    def eliminate(b):
        first = b * 8
        old = inverse[pl.ds(pl.multiple_of(first, 8), 8), :]
        panel = old
        for r in range(8):
            at = lane8 == first + r
            column = cols_sum(jnp.where(at, panel, 0.0))
            panel = jnp.where(at, jnp.where(sub8 == r, 1.0, 0.0), panel)
            pivot = panel[r : r + 1, :] / column[r : r + 1, :]
            panel = jnp.where(sub8 == r, pivot, panel - column * pivot)
        done = lane8 < first
        within = (lane8 >= first) & (lane8 < first + 8)
        left = jnp.where(within, 0.0, jnp.where(done, -old, old))
        change = lax.dot_general(
            left, panel, (((0,), (0,)), ((), ())), precision=HIGHEST, preferred_element_type=F32
        )
        inside = (lane_all >= first) & (lane_all < first + 8)
        inverse[...] = jnp.where(inside, 0.0, inverse[...]) - change
        inverse[pl.ds(pl.multiple_of(first, 8), 8), :] = panel

    serve(0, own)
    forward(1)
    serve(1, right1)
    serve(2, left1)

    each(1, Y, lambda e: gram_y_copy(e).wait_recv())
    total = gram_y[0]
    for i in range(1, Y):
        total = total + gram_y[i]
    gram_mine[...] = total

    def gram_x_copy(d):
        return to(gram_mine, gram_x.at[q], gx_s.at[d], gx_r.at[d], x_peer(d))

    each(1, X, lambda d: gram_x_copy(d).start())
    gram_x[q] = total
    load_tiles.wait()
    contribute(0)

    forward(2)
    serve(3, right2)
    serve(4, left2)

    each(1, X, lambda d: gram_x_copy(d).wait_recv())
    total = gram_x[0]
    for i in range(1, X):
        total = total + gram_x[i]
    gram_sum[...] = total

    def gram_g_copy(e):
        return to(gram_sum, gram.at[y], gg_s.at[e], gg_r.at[e], y_peer(e))

    each(1, Y, lambda e: gram_g_copy(e).start())
    gram[y] = total
    contribute(1)

    forward(3)
    serve(5, right3)
    serve(6, left3)
    contribute(2)

    each(1, Y, lambda e: gram_g_copy(e).wait_recv())
    gram_day = lax.dot_general(
        day_ref[...], day_ref[...], (((0,), (0,)), ((), ())), preferred_element_type=F32
    )
    inverse[...] = gram[...].reshape(RANK, RANK) * gram_day

    ring(0, 3, 0).wait_recv()
    ring(1, 3, 1).wait_recv()
    serve(7, far)
    contribute(3)
    contribute(4)
    each(0, 8, eliminate)
    contribute(5)
    contribute(6)
    contribute(7)

    def add(r, run):
        run = contribs[plan_s[1, r] & 63] + jnp.where(plan_s[2, r] == 1, run, 0.0)
        sums[r] = run
        return run

    lax.fori_loop(0, 64, add, jnp.zeros((TS, RANK), F32))

    def pick(i):
        for j in range(2):
            p = 2 * i + j
            end = plan_s[3, p]
            value = sums[jnp.maximum(end - 1, 0) & 63]
            value = jnp.where(end > plan_s[4, p], value, 0.0).astype(jnp.bfloat16)
            for part in range(4):
                send_x[4 * j + part, i] = value[16 * part : 16 * part + 16]

    each(0, 8, pick)

    def rx_copy(d):
        return to(send_x.at[(q + d) % X], recv_x.at[d], rx_s.at[d], rx_r.at[d], x_peer(d))

    each(1, X, lambda d: rx_copy(d).start())
    each(8, 12, eliminate)
    each(1, X, lambda d: rx_copy(d).wait_recv())
    share = send_x[q].astype(F32)
    for d in range(1, X):
        share = share + recv_x[d].astype(F32)
    send_y[...] = share.astype(jnp.bfloat16)

    def ry_copy(e):
        return to(send_y.at[(y + e) % Y], recv_y.at[e], ry_s.at[e], ry_r.at[e], y_peer(e))

    each(1, Y, lambda e: ry_copy(e).start())
    each(12, 16, eliminate)
    each(1, Y, lambda e: ry_copy(e).wait_recv())
    mine = send_y[y].astype(F32)
    for e in range(1, Y):
        mine = mine + recv_y[e].astype(F32)
    out_ref[...] = jnp.dot(mine, inverse[...], precision=HIGHEST, preferred_element_type=F32)

    for direction in range(2):
        for step in range(4):
            for part in range(2):
                if step < 3 or part == direction:
                    ring(direction, step, part).wait_send()
    for k in range(8):
        each(1, X, lambda d: block_copy(k, d).wait_send())

    def sent(d):
        list_copy(d).wait_send()
        gram_y_copy(d).wait_send()
        gram_x_copy(d).wait_send()
        gram_g_copy(d).wait_send()
        rx_copy(d).wait_send()
        ry_copy(d).wait_send()

    each(1, 8, sent)


def local(tiles, tile_blocks, counts, fetch_list, store_factor, day_factor):
    blocks = tile_blocks[0].T
    fetch = fetch_list.reshape(1, -1)
    store = store_factor.reshape(SB, TS, RANK)
    vmem = pl.BlockSpec(memory_space=pltpu.VMEM)
    hbm = pl.BlockSpec(memory_space=pl.ANY)
    bf16 = jnp.bfloat16
    dma = pltpu.SemaphoreType.DMA
    ring_buf = pltpu.VMEM((SB, TS, RANK), bf16)
    return pl.pallas_call(
        kernel,
        out_shape=jax.ShapeDtypeStruct((16, RANK), F32),
        in_specs=[hbm, vmem, pl.BlockSpec(memory_space=pltpu.SMEM), vmem, hbm, vmem],
        out_specs=vmem,
        scratch_shapes=[
            pltpu.VMEM(tiles.shape, bf16),
            ring_buf, ring_buf, ring_buf, ring_buf, ring_buf, ring_buf, ring_buf, ring_buf,
            pltpu.VMEM((Y, X, TS, RANK), bf16),
            pltpu.VMEM((Y, X, TS, RANK), bf16),
            pltpu.VMEM((X * Y, 64, RANK), F32),
            pltpu.VMEM((64, 64, RANK), F32),
            pltpu.VMEM((8, 128), jnp.int32),
            pltpu.SMEM((8, 128), jnp.int32),
            pltpu.VMEM((8, 128), jnp.int32),
            pltpu.VMEM((X, 8, 128), jnp.int32),
            pltpu.SMEM((X, 8, 128), jnp.int32),
            pltpu.VMEM((RANK, RANK), F32),
            pltpu.VMEM((Y, 16, RANK), F32),
            pltpu.VMEM((16, RANK), F32),
            pltpu.VMEM((X, 16, RANK), F32),
            pltpu.VMEM((16, RANK), F32),
            pltpu.VMEM((Y, 16, RANK), F32),
            pltpu.VMEM((RANK, RANK), F32),
            pltpu.VMEM((X, Y, 16, RANK), bf16),
            pltpu.VMEM((X, Y, 16, RANK), bf16),
            pltpu.VMEM((Y, 16, RANK), bf16),
            pltpu.VMEM((Y, 16, RANK), bf16),
            dma((4,)),
            dma((2, 4, 2)), dma((2, 4, 2)),
            dma((8,)), dma((8,)),
            dma((8, 8)), dma((8, 8)),
            dma((8,)), dma((8,)), dma((8,)), dma((8,)), dma((8,)), dma((8,)),
            dma((8,)), dma((8,)), dma((8,)), dma((8,)),
        ],
        compiler_params=pltpu.CompilerParams(
            collective_id=0, has_side_effects=True, vmem_limit_bytes=60 * 1024 * 1024
        ),
    )(tiles, blocks, counts, fetch, store, day_factor)


def solution(mesh):
    return jax.shard_map(
        local,
        mesh=mesh,
        in_specs=(
            P(("prod", "store"), None, None),
            P(("prod", "store"), None, None),
            P(("prod", "store")),
            P(("prod", "store"), None, None),
            P("store", None),
            P(),
        ),
        out_specs=P(("prod", "store"), None),
        check_vma=False,
    )
```

```python
import jax
import jax.numpy as jnp
from jax import lax
from jax.experimental import pallas as pl
from jax.experimental.pallas import tpu as pltpu
from jax.sharding import PartitionSpec as P

PB = 16
SB = 8
TS = 64
RANK = 128
DAYS = 8
X = 8
Y = 8
HIGHEST = lax.Precision.HIGHEST
F32 = jnp.float32


def rows_sum(x):
    return jnp.sum(x, axis=0, keepdims=True)


def cols_sum(x):
    return jnp.sum(x, axis=1, keepdims=True)


def plan(blocks, count):
    slots = blocks.shape[1]
    sub = lax.broadcasted_iota(jnp.int32, (slots, slots), 0)
    lane = lax.broadcasted_iota(jnp.int32, (slots, slots), 1)
    lane_row = lax.broadcasted_iota(jnp.int32, (1, slots), 1)
    p_row, perm_row = blocks[0:1, :], blocks[1:2, :]
    key_row = jnp.where(lane_row < count, p_row * slots, PB * slots * 4) + perm_row
    eye = sub == lane
    perm_col = cols_sum(jnp.where(eye, perm_row, 0))
    key_col = cols_sum(jnp.where(eye, key_row, 0))
    rank_col = cols_sum(jnp.where(key_row < key_col, 1, 0))
    tile_of = rows_sum(jnp.where(perm_col == lane, sub, 0))
    order = rows_sum(jnp.where(rank_col == lane, perm_col, 0))
    block_at = rows_sum(jnp.where(rank_col == lane, key_col // slots, 0))
    block_before = rows_sum(jnp.where(rank_col + 1 == lane, key_col // slots, 0))
    same = jnp.where((block_at == block_before) & (lane_row > 0), 1, 0)
    ends = rows_sum(jnp.where(key_col < (lane + 1) * slots, 1, 0))
    begins = rows_sum(jnp.where(key_col < lane * slots, 1, 0))
    return tile_of, order, same, ends, begins


def kernel(
    tiles_hbm, blocks_hbm, count_ref, fetch_hbm, store_hbm, day_hbm, out_ref,
    blocks_ref, fetch_ref, day_ref, tiles, own, right1, right2, right3, left1, left2, left3, far,
    table, stage, contribs, sums,
    plan_v, plan_s, my_list, lists_v, lists_s,
    gram_part, gram_x, gram_sum, gram, inverse,
    send_x, recv_x, send_y, recv_y,
    local_sem, ring_s, ring_r, list_s, list_r, block_s, block_r,
    gx_s, gx_r, gg_s, gg_r, rx_s, rx_r, ry_s, ry_r,
):
    me = lax.axis_index("store")
    y, q = me // X, me % X

    def x_peer(d):
        return y * X + (q + d) % X

    def y_peer(e):
        return (y + e) % Y * X + q

    def to(src, dst, send, recv, target):
        return pltpu.make_async_remote_copy(
            src_ref=src, dst_ref=dst, send_sem=send, recv_sem=recv,
            device_id={"store": target}, device_id_type=pl.DeviceIdType.MESH,
        )

    def each(first, last, body, unroll=1):
        def step(i, carry):
            body(i)
            return carry
        lax.fori_loop(first, last, step, 0, unroll=unroll)

    barrier = pltpu.get_barrier_semaphore()

    def greet(target):
        pl.semaphore_signal(
            barrier, inc=1, device_id={"store": target}, device_id_type=pl.DeviceIdType.MESH)

    def load(src, dst, i):
        copy = pltpu.make_async_copy(src, dst, local_sem.at[i])
        copy.start()
        return copy

    greet(y_peer(1))
    greet(y_peer(Y - 1))
    each(1, X, lambda d: greet(x_peer(d)))
    load_fetch = load(fetch_hbm, fetch_ref, 0)
    load_own = load(store_hbm, own, 1)
    load_blocks = load(blocks_hbm, blocks_ref, 2)
    load_day = load(day_hbm, day_ref, 3)
    load_tiles = load(tiles_hbm, tiles, 4)
    load_fetch.wait()
    my_list[0:1, 0:64] = fetch_ref[...]
    load_own.wait()
    pl.semaphore_wait(barrier, X + 1)

    def list_copy(d):
        return to(
            my_list.at[0:1], lists_v.at[d, 0:1], list_s.at[d], list_r.at[d], x_peer(d)
        )

    each(1, X, lambda d: list_copy(d).start())

    rights, lefts = [right1, right2, right3, far], [left1, left2, left3, far]
    parts, size = 4, SB // 4

    def ring(direction, step, part):
        bufs = rights if direction == 0 else lefts
        src = own if step == 0 else bufs[step - 1]
        cut = pl.ds(part * size, size)
        return to(
            src.at[cut], bufs[step].at[cut],
            ring_s.at[direction, step, part], ring_r.at[direction, step, part],
            y_peer(1 if direction == 0 else Y - 1),
        )

    for part in range(parts):
        ring(0, 0, part).start()
        ring(1, 0, part).start()

    def gram_add(*bufs):
        total = None
        for buf in bufs:
            rows = buf[...].reshape(SB * TS, RANK)
            part = lax.dot_general(
                rows, rows, (((0,), (0,)), ((), ())), preferred_element_type=F32
            )
            total = part if total is None else total + part
        return total

    load_blocks.wait()
    for row, value in enumerate(plan(blocks_ref[...], count_ref[0])):
        plan_v[row : row + 1, 0:64] = value
    load_plan = load(plan_v, plan_s, 5)
    lists_v[0, 0:1] = my_list[0:1]


    def block_copy(k, d):
        return to(stage.at[k, d], table.at[k, d], block_s.at[k, d], block_r.at[k, d], x_peer(d))

    def owner(k, d):
        shift = (0, Y - 1, 1, Y - 2, 2, Y - 3, 3, 4)[k]
        return (y + shift) % Y * X + (q + X - d) % X

    def serve(k, buf):
        mine = owner(k, 0)
        table[k, 0] = buf[lists_s[0, 0, mine] & (SB - 1)]

        def one(d):
            stage[k, d] = buf[lists_s[X - d, 0, mine] & (SB - 1)]
            block_copy(k, d).start()

        each(1, X, one)

    load_day.wait()
    day = day_ref[...].astype(F32)

    def contribute(k):
        def one(d):
            entry = owner(k, d)
            rows = table[k, d].astype(F32)
            kron = (rows[:, None, :] * day[None, :, :]).reshape(TS * DAYS, RANK).astype(jnp.bfloat16)
            contribs[entry] = jnp.dot(
                tiles[plan_s[0, entry] & 63], kron, preferred_element_type=F32
            )

        each(1, X, lambda d: block_copy(k, d).wait_recv())
        each(0, X, one, unroll=4)

    def forward(step):
        for part in range(parts):
            for direction in range(2):
                ring(direction, step - 1, part).wait_recv()
                if step < 3 or part // 2 == direction:
                    ring(direction, step, part).start()

    lane8 = lax.broadcasted_iota(jnp.int32, (8, RANK), 1)
    sub8 = lax.broadcasted_iota(jnp.int32, (8, RANK), 0)
    lane_all = lax.broadcasted_iota(jnp.int32, (RANK, RANK), 1)
    sub_all = lax.broadcasted_iota(jnp.int32, (RANK, RANK), 0)

    def lane_of(rows, at):
        return jnp.broadcast_to(cols_sum(jnp.where(lane8 == at, rows, 0.0)), (8, RANK))

    def sub_of(rows, r):
        return jnp.broadcast_to(rows[r : r + 1, :], (8, RANK))

    def invert8(rows, first):
        columns = [lane_of(rows, first + r) for r in range(8)]
        d = {(i, j): sub_of(columns[j], i) for j in range(8) for i in range(j + 1)}
        for k in range(8):
            recip = 1.0 / d[k, k]
            row = [d[min(i, k), max(i, k)] for i in range(8)]
            scaled = [x * recip for x in row]
            for j in range(8):
                for i in range(j + 1):
                    if i != k and j != k:
                        d[i, j] = d[i, j] - scaled[i] * row[j]
            for i in range(8):
                if i != k:
                    d[min(i, k), max(i, k)] = scaled[i]
            d[k, k] = -recip
        out = []
        for r in range(8):
            column = -d[r, 7]
            for i in range(7):
                column = jnp.where(sub8 == i, -d[min(i, r), max(i, r)], column)
            out.append(column)
        return out

    def gj_apply(left, done_rows, first):
        change = lax.dot_general(
            left, done_rows, (((0,), (0,)), ((), ())), precision=HIGHEST, preferred_element_type=F32
        )
        inside = (lane_all >= first) & (lane_all < first + 8)
        rows_in = (sub_all >= first) & (sub_all < first + 8)
        new = jnp.where(inside, 0.0, inverse[...]) - change
        inverse[...] = jnp.where(rows_in, jnp.broadcast_to(done_rows[None], (16, 8, RANK)).reshape(RANK, RANK), new)

    def gj_start():
        zero = jnp.zeros((8, RANK), F32)
        return inverse[0:8, :], zero, zero

    def gj_step(b, state):
        rows, left, done_rows = state
        first = b * 8
        gj_apply(left, done_rows, first - 8)
        within = (lane8 >= first) & (lane8 < first + 8)
        columns = invert8(rows, first)
        unit = jnp.where(within, jnp.where(lane8 - first == sub8, 1.0, 0.0), rows)
        new = columns[0] * sub_of(unit, 0)
        for r in range(1, 8):
            new = new + columns[r] * sub_of(unit, r)
        new_left = jnp.where(within, 0.0, jnp.where(lane8 < first, -rows, rows))
        after = inverse[pl.ds(pl.multiple_of(jnp.minimum(first + 8, RANK - 8), 8), 8), :]
        step = lane_of(after, first) * sub_of(new, 0)
        for r in range(1, 8):
            step = step + lane_of(after, first + r) * sub_of(new, r)
        return jnp.where(within, 0.0, after) - step, new_left, new

    def gj_end(state):
        gj_apply(state[1], state[2], RANK - 8)

    gram_part[...] = gram_add(own)
    forward(1)
    each(1, X, lambda d: list_copy(d).wait_recv())
    load(lists_v, lists_s, 6).wait()
    serve(0, own)
    serve(1, right1)
    serve(2, left1)
    gram_part[...] += gram_add(right1, left1)
    forward(2)
    serve(3, right2)
    serve(4, left2)
    gram_part[...] += gram_add(right2, left2)
    forward(3)
    serve(5, right3)
    serve(6, left3)
    gram_part[...] += gram_add(right3, left3)
    for part in range(2):
        ring(0, 3, part).wait_recv()
        ring(1, 3, 2 + part).wait_recv()
    serve(7, far)
    gram_part[...] += gram_add(far)

    gram_x[q] = gram_part[pl.ds(y * 16, 16), :]

    def gram_x_copy(d):
        return to(
            gram_part.at[pl.ds(y * 16, 16)], gram_x.at[q], gx_s.at[d], gx_r.at[d], x_peer(d)
        )

    def gram_g_copy(e):
        return to(gram_sum, gram.at[y], gg_s.at[e], gg_r.at[e], y_peer(e))

    each(1, X, lambda d: gram_x_copy(d).start())
    load_tiles.wait()
    load_plan.wait()
    for k in range(5):
        contribute(k)
    each(1, X, lambda d: gram_x_copy(d).wait_recv())
    total = gram_x[0]
    for i in range(1, X):
        total = total + gram_x[i]
    gram_sum[...] = total
    gram[y] = total
    each(1, Y, lambda e: gram_g_copy(e).start())
    contribute(5)
    contribute(6)
    contribute(7)

    def add(r, run):
        run = contribs[plan_s[1, r] & 63] + jnp.where(plan_s[2, r] == 1, run, 0.0)
        sums[r] = run
        return run

    lax.fori_loop(0, 64, add, jnp.zeros((TS, RANK), F32), unroll=8)

    def pick(i):
        place = (i + Y - y + 5) % Y
        for j in range(2):
            p = 2 * i + j
            end = plan_s[3, p]
            value = sums[jnp.maximum(end - 1, 0) & 63]
            value = jnp.where(end > plan_s[4, p], value, 0.0).astype(jnp.bfloat16)
            for part in range(4):
                send_x[4 * j + part, place] = value[16 * part : 16 * part + 16]

    each(0, 8, pick, unroll=2)

    cuts = (pl.ds(0, 3), pl.ds(3, 5))

    def rx_copy(d, part):
        return to(
            send_x.at[(q + d) % X, cuts[part]], recv_x.at[d, cuts[part]],
            rx_s.at[part, d], rx_r.at[part, d], x_peer(d),
        )

    def ry_copy(e):
        return to(send_y.at[(e + 5) % Y], recv_y.at[e], ry_s.at[e], ry_r.at[e], y_peer(e))

    def sum_x(part):
        each(1, X, lambda d: rx_copy(d, part).wait_recv())
        share = send_x[q, cuts[part]].astype(F32)
        for d in range(1, X):
            share = share + recv_x[d, cuts[part]].astype(F32)
        send_y[cuts[part]] = share.astype(jnp.bfloat16)

    for part in range(2):
        each(1, X, lambda d: rx_copy(d, part).start())
    each(1, Y, lambda e: gram_g_copy(e).wait_recv())
    gram_day = lax.dot_general(
        day_ref[...], day_ref[...], (((0,), (0,)), ((), ())), preferred_element_type=F32
    )
    inverse[...] = gram[...].reshape(RANK, RANK) * gram_day
    state = lax.fori_loop(0, 8, gj_step, gj_start())
    sum_x(0)
    each(3, 6, lambda e: ry_copy(e).start())
    state = lax.fori_loop(8, 10, gj_step, state)
    sum_x(1)
    each(1, 3, lambda e: ry_copy(e).start())
    each(6, 8, lambda e: ry_copy(e).start())
    gj_end(lax.fori_loop(10, 16, gj_step, state))

    for direction in range(2):
        for step in range(4):
            for part in range(parts):
                if step < 3 or part // 2 == direction:
                    ring(direction, step, part).wait_send()
    for k in range(8):
        each(1, X, lambda d: block_copy(k, d).wait_send())

    def sent(d):
        list_copy(d).wait_send()
        gram_x_copy(d).wait_send()
        gram_g_copy(d).wait_send()
        rx_copy(d, 0).wait_send()
        rx_copy(d, 1).wait_send()

    each(1, 8, sent)

    each(1, Y, lambda e: ry_copy(e).wait_recv())
    mine = send_y[5].astype(F32)
    for e in range(1, Y):
        mine = mine + recv_y[e].astype(F32)
    each(1, Y, lambda e: ry_copy(e).wait_send())
    out_ref[...] = jnp.dot(mine, inverse[...], precision=HIGHEST, preferred_element_type=F32)


def local(tiles, tile_blocks, counts, fetch_list, store_factor, day_factor):
    blocks = tile_blocks[0].T
    fetch = fetch_list.reshape(1, -1)
    store = store_factor.reshape(SB, TS, RANK)
    vmem = pl.BlockSpec(memory_space=pltpu.VMEM)
    hbm = pl.BlockSpec(memory_space=pl.ANY)
    bf16 = jnp.bfloat16
    dma = pltpu.SemaphoreType.DMA
    ring_buf = pltpu.VMEM((SB, TS, RANK), bf16)
    return pl.pallas_call(
        kernel,
        out_shape=jax.ShapeDtypeStruct((16, RANK), F32),
        in_specs=[hbm, hbm, pl.BlockSpec(memory_space=pltpu.SMEM), hbm, hbm, hbm],
        out_specs=vmem,
        scratch_shapes=[
            pltpu.VMEM(blocks.shape, jnp.int32), pltpu.VMEM(fetch.shape, jnp.int32), pltpu.VMEM(day_factor.shape, bf16),
            pltpu.VMEM(tiles.shape, bf16),
            ring_buf, ring_buf, ring_buf, ring_buf, ring_buf, ring_buf, ring_buf, ring_buf,
            pltpu.VMEM((Y, X, TS, RANK), bf16),
            pltpu.VMEM((Y, X, TS, RANK), bf16),
            pltpu.VMEM((X * Y, 64, RANK), F32),
            pltpu.VMEM((64, 64, RANK), F32),
            pltpu.VMEM((8, 128), jnp.int32),
            pltpu.SMEM((8, 128), jnp.int32),
            pltpu.VMEM((8, 128), jnp.int32),
            pltpu.VMEM((X, 8, 128), jnp.int32),
            pltpu.SMEM((X, 8, 128), jnp.int32),
            pltpu.VMEM((RANK, RANK), F32),
            pltpu.VMEM((X, 16, RANK), F32),
            pltpu.VMEM((16, RANK), F32),
            pltpu.VMEM((Y, 16, RANK), F32),
            pltpu.VMEM((RANK, RANK), F32),
            pltpu.VMEM((X, Y, 16, RANK), bf16),
            pltpu.VMEM((X, Y, 16, RANK), bf16),
            pltpu.VMEM((Y, 16, RANK), bf16),
            pltpu.VMEM((Y, 16, RANK), bf16),
            dma((8,)),
            dma((2, 4, 4)), dma((2, 4, 4)),
            dma((8,)), dma((8,)),
            dma((8, 8)), dma((8, 8)),
            dma((8,)), dma((8,)), dma((8,)), dma((8,)),
            dma((2, 8)), dma((2, 8)), dma((8,)), dma((8,)),
        ],
        compiler_params=pltpu.CompilerParams(
            collective_id=0, has_side_effects=True, vmem_limit_bytes=60 * 1024 * 1024
        ),
    )(tiles, blocks, counts, fetch, store, day_factor)


def solution(mesh):
    return jax.shard_map(
        local,
        mesh=mesh,
        in_specs=(
            P(("prod", "store"), None, None),
            P(("prod", "store"), None, None),
            P(("prod", "store")),
            P(("prod", "store"), None, None),
            P("store", None),
            P(),
        ),
        out_specs=P(("prod", "store"), None),
        check_vma=False,
    )
```

```python
import jax
import jax.numpy as jnp
from jax import lax
from jax.experimental import pallas as pl
from jax.experimental.pallas import tpu as pltpu
from jax.sharding import PartitionSpec as P

PB = 16
SB = 8
TS = 64
RANK = 128
DAYS = 8
X = 8
Y = 8
HIGHEST = lax.Precision.HIGHEST
F32 = jnp.float32


def rows_sum(x):
    return jnp.sum(x, axis=0, keepdims=True)


def cols_sum(x):
    return jnp.sum(x, axis=1, keepdims=True)


def plan(blocks, count):
    slots = blocks.shape[1]
    sub = lax.broadcasted_iota(jnp.int32, (slots, slots), 0)
    lane = lax.broadcasted_iota(jnp.int32, (slots, slots), 1)
    lane_row = lax.broadcasted_iota(jnp.int32, (1, slots), 1)
    p_row, perm_row = blocks[0:1, :], blocks[1:2, :]
    key_row = jnp.where(lane_row < count, p_row * slots, PB * slots * 4) + perm_row
    eye = sub == lane
    perm_col = cols_sum(jnp.where(eye, perm_row, 0))
    key_col = cols_sum(jnp.where(eye, key_row, 0))
    rank_col = cols_sum(jnp.where(key_row < key_col, 1, 0))
    tile_of = rows_sum(jnp.where(perm_col == lane, sub, 0))
    order = rows_sum(jnp.where(rank_col == lane, perm_col, 0))
    block_at = rows_sum(jnp.where(rank_col == lane, key_col // slots, 0))
    block_before = rows_sum(jnp.where(rank_col + 1 == lane, key_col // slots, 0))
    same = jnp.where((block_at == block_before) & (lane_row > 0), 1, 0)
    ends = rows_sum(jnp.where(key_col < (lane + 1) * slots, 1, 0))
    begins = rows_sum(jnp.where(key_col < lane * slots, 1, 0))
    return tile_of, order, same, ends, begins


def kernel(
    tiles_hbm, blocks_hbm, count_ref, fetch_hbm, store_hbm, day_hbm, out_ref,
    blocks_ref, fetch_ref, day_ref, tiles, own, right1, right2, right3, left1, left2, left3, far,
    table, stage, contribs, sums,
    plan_v, plan_s, my_list, lists_v, lists_s,
    gram_part, gram_x, gram_sum, gram, inverse,
    send_x, recv_x, send_y, recv_y,
    local_sem, ring_s, ring_r, list_s, list_r, block_s, block_r,
    gx_s, gx_r, gg_s, gg_r, rx_s, rx_r, ry_s, ry_r,
):
    me = lax.axis_index("store")
    y, q = me // X, me % X

    def x_peer(d):
        return y * X + (q + d) % X

    def y_peer(e):
        return (y + e) % Y * X + q

    def to(src, dst, send, recv, target):
        return pltpu.make_async_remote_copy(
            src_ref=src, dst_ref=dst, send_sem=send, recv_sem=recv,
            device_id={"store": target}, device_id_type=pl.DeviceIdType.MESH,
        )

    def group_wait(ref, sem):
        pltpu.make_async_copy(ref, ref, sem).wait()

    def each(first, last, body, unroll=1):
        def step(i, carry):
            body(i)
            return carry
        lax.fori_loop(first, last, step, 0, unroll=unroll)

    barrier = pltpu.get_barrier_semaphore()

    def greet(target):
        pl.semaphore_signal(
            barrier, inc=1, device_id={"store": target}, device_id_type=pl.DeviceIdType.MESH)

    def load(src, dst, i):
        copy = pltpu.make_async_copy(src, dst, local_sem.at[i])
        copy.start()
        return copy

    greet(y_peer(1))
    greet(y_peer(Y - 1))
    each(1, X, lambda d: greet(x_peer(d)))
    load_fetch = load(fetch_hbm, fetch_ref, 0)
    load_own = load(store_hbm, own, 1)
    load_blocks = load(blocks_hbm, blocks_ref, 2)
    load_day = load(day_hbm, day_ref, 3)
    load_tiles = load(tiles_hbm, tiles, 4)
    load_fetch.wait()
    my_list[0:1, 0:64] = fetch_ref[...]
    load_own.wait()
    pl.semaphore_wait(barrier, X + 1)

    def list_copy(d):
        return to(
            my_list.at[0:1], lists_v.at[d, 0:1], list_s, list_r, x_peer(d)
        )

    each(1, X, lambda d: list_copy(d).start())

    rights, lefts = [right1, right2, right3, far], [left1, left2, left3, far]
    parts, size = 4, SB // 4

    def ring(direction, step, part):
        bufs = rights if direction == 0 else lefts
        src = own if step == 0 else bufs[step - 1]
        cut = pl.ds(part * size, size)
        return to(
            src.at[cut], bufs[step].at[cut],
            ring_s.at[direction, step], ring_r.at[direction, step, part],
            y_peer(1 if direction == 0 else Y - 1),
        )

    for part in range(parts):
        ring(0, 0, part).start()
        ring(1, 0, part).start()

    def gram_add(*bufs):
        total = None
        for buf in bufs:
            rows = buf[...].reshape(SB * TS, RANK)
            part = lax.dot_general(
                rows, rows, (((0,), (0,)), ((), ())), preferred_element_type=F32
            )
            total = part if total is None else total + part
        return total

    load_blocks.wait()
    for row, value in enumerate(plan(blocks_ref[...], count_ref[0])):
        plan_v[row : row + 1, 0:64] = value
    load_plan = load(plan_v, plan_s, 5)
    lists_v[0, 0:1] = my_list[0:1]


    def block_copy(k, d):
        return to(stage.at[k, d], table.at[k, d], block_s.at[k], block_r.at[k], x_peer(d))

    def owner(k, d):
        shift = (0, Y - 1, 1, Y - 2, 2, Y - 3, 3, 4)[k]
        return (y + shift) % Y * X + (q + X - d) % X

    def serve(k, buf):
        mine = owner(k, 0)
        table[k, 0] = buf[lists_s[0, 0, mine] & (SB - 1)]

        def one(d):
            stage[k, d] = buf[lists_s[X - d, 0, mine] & (SB - 1)]
            block_copy(k, d).start()

        each(1, X, one)

    load_day.wait()
    day = day_ref[...].astype(F32)

    def contribute(k):
        def one(d):
            entry = owner(k, d)
            rows = table[k, d].astype(F32)
            kron = (rows[:, None, :] * day[None, :, :]).reshape(TS * DAYS, RANK).astype(jnp.bfloat16)
            contribs[entry] = jnp.dot(
                tiles[plan_s[0, entry] & 63], kron, preferred_element_type=F32
            )

        group_wait(table.at[k, pl.ds(1, X - 1)], block_r.at[k])
        each(0, X, one, unroll=4)

    def forward(step):
        for part in range(parts):
            for direction in range(2):
                ring(direction, step - 1, part).wait_recv()
                if step < 3 or part // 2 == direction:
                    ring(direction, step, part).start()

    lane8 = lax.broadcasted_iota(jnp.int32, (8, RANK), 1)
    sub8 = lax.broadcasted_iota(jnp.int32, (8, RANK), 0)
    lane_all = lax.broadcasted_iota(jnp.int32, (RANK, RANK), 1)
    sub_all = lax.broadcasted_iota(jnp.int32, (RANK, RANK), 0)

    def lane_of(rows, at):
        return jnp.broadcast_to(cols_sum(jnp.where(lane8 == at, rows, 0.0)), (8, RANK))

    def sub_of(rows, r):
        return jnp.broadcast_to(rows[r : r + 1, :], (8, RANK))

    def invert8(rows, first):
        columns = [lane_of(rows, first + r) for r in range(8)]
        d = {(i, j): sub_of(columns[j], i) for j in range(8) for i in range(j + 1)}
        for k in range(8):
            recip = 1.0 / d[k, k]
            row = [d[min(i, k), max(i, k)] for i in range(8)]
            scaled = [x * recip for x in row]
            for j in range(8):
                for i in range(j + 1):
                    if i != k and j != k:
                        d[i, j] = d[i, j] - scaled[i] * row[j]
            for i in range(8):
                if i != k:
                    d[min(i, k), max(i, k)] = scaled[i]
            d[k, k] = -recip
        out = []
        for r in range(8):
            column = -d[r, 7]
            for i in range(7):
                column = jnp.where(sub8 == i, -d[min(i, r), max(i, r)], column)
            out.append(column)
        return out

    def gj_apply(left, done_rows, first):
        change = lax.dot_general(
            left, done_rows, (((0,), (0,)), ((), ())), precision=HIGHEST, preferred_element_type=F32
        )
        inside = (lane_all >= first) & (lane_all < first + 8)
        rows_in = (sub_all >= first) & (sub_all < first + 8)
        new = jnp.where(inside, 0.0, inverse[...]) - change
        inverse[...] = jnp.where(rows_in, jnp.broadcast_to(done_rows[None], (16, 8, RANK)).reshape(RANK, RANK), new)

    def gj_start():
        zero = jnp.zeros((8, RANK), F32)
        return inverse[0:8, :], zero, zero

    def gj_step(b, state):
        rows, left, done_rows = state
        first = b * 8
        gj_apply(left, done_rows, first - 8)
        within = (lane8 >= first) & (lane8 < first + 8)
        columns = invert8(rows, first)
        unit = jnp.where(within, jnp.where(lane8 - first == sub8, 1.0, 0.0), rows)
        new = columns[0] * sub_of(unit, 0)
        for r in range(1, 8):
            new = new + columns[r] * sub_of(unit, r)
        new_left = jnp.where(within, 0.0, jnp.where(lane8 < first, -rows, rows))
        after = inverse[pl.ds(pl.multiple_of(jnp.minimum(first + 8, RANK - 8), 8), 8), :]
        step = lane_of(after, first) * sub_of(new, 0)
        for r in range(1, 8):
            step = step + lane_of(after, first + r) * sub_of(new, r)
        return jnp.where(within, 0.0, after) - step, new_left, new

    def gj_end(state):
        gj_apply(state[1], state[2], RANK - 8)

    gram_part[...] = gram_add(own)
    forward(1)
    group_wait(lists_v.at[pl.ds(1, X - 1), 0:1], list_r)
    load(lists_v, lists_s, 6).wait()
    serve(0, own)
    serve(1, right1)
    serve(2, left1)
    gram_part[...] += gram_add(right1, left1)
    forward(2)
    serve(3, right2)
    serve(4, left2)
    gram_part[...] += gram_add(right2, left2)
    forward(3)
    serve(5, right3)
    serve(6, left3)
    gram_part[...] += gram_add(right3, left3)
    for part in range(2):
        ring(0, 3, part).wait_recv()
        ring(1, 3, 2 + part).wait_recv()
    serve(7, far)
    gram_part[...] += gram_add(far)

    gram_x[q] = gram_part[pl.ds(y * 16, 16), :]

    def gram_x_copy(d):
        return to(
            gram_part.at[pl.ds(y * 16, 16)], gram_x.at[q], gx_s, gx_r, x_peer(d)
        )

    def gram_g_copy(e):
        return to(gram_sum, gram.at[y], gg_s, gg_r, y_peer(e))

    each(1, X, lambda d: gram_x_copy(d).start())
    load_tiles.wait()
    load_plan.wait()
    for k in range(5):
        contribute(k)
    group_wait(gram_x.at[pl.ds(0, X - 1)], gx_r)
    total = gram_x[0]
    for i in range(1, X):
        total = total + gram_x[i]
    gram_sum[...] = total
    gram[y] = total
    each(1, Y, lambda e: gram_g_copy(e).start())
    contribute(5)
    contribute(6)
    contribute(7)

    def add(r, run):
        run = contribs[plan_s[1, r] & 63] + jnp.where(plan_s[2, r] == 1, run, 0.0)
        sums[r] = run
        return run

    lax.fori_loop(0, 64, add, jnp.zeros((TS, RANK), F32), unroll=8)

    def pick(i):
        place = (i + Y - y + 5) % Y
        for j in range(2):
            p = 2 * i + j
            end = plan_s[3, p]
            value = sums[jnp.maximum(end - 1, 0) & 63]
            value = jnp.where(end > plan_s[4, p], value, 0.0).astype(jnp.bfloat16)
            for part in range(4):
                send_x[4 * j + part, place] = value[16 * part : 16 * part + 16]

    each(0, 8, pick, unroll=2)

    cuts = (pl.ds(0, 3), pl.ds(3, 5))

    def rx_copy(d, part):
        return to(
            send_x.at[(q + d) % X, cuts[part]], recv_x.at[d, cuts[part]],
            rx_s.at[part], rx_r.at[part], x_peer(d),
        )

    def ry_copy(e):
        return to(send_y.at[(e + 5) % Y], recv_y.at[e], ry_s, ry_r, y_peer(e))

    def sum_x(part):
        group_wait(recv_x.at[pl.ds(1, X - 1), cuts[part]], rx_r.at[part])
        share = send_x[q, cuts[part]].astype(F32)
        for d in range(1, X):
            share = share + recv_x[d, cuts[part]].astype(F32)
        send_y[cuts[part]] = share.astype(jnp.bfloat16)

    for part in range(2):
        each(1, X, lambda d: rx_copy(d, part).start())
    group_wait(gram.at[pl.ds(0, Y - 1)], gg_r)
    gram_day = lax.dot_general(
        day_ref[...], day_ref[...], (((0,), (0,)), ((), ())), preferred_element_type=F32
    )
    inverse[...] = gram[...].reshape(RANK, RANK) * gram_day
    state = lax.fori_loop(0, 8, gj_step, gj_start())
    sum_x(0)
    each(3, 6, lambda e: ry_copy(e).start())
    state = lax.fori_loop(8, 10, gj_step, state)
    sum_x(1)
    each(1, 3, lambda e: ry_copy(e).start())
    each(6, 8, lambda e: ry_copy(e).start())
    gj_end(lax.fori_loop(10, 16, gj_step, state))

    for direction in range(2):
        for step in range(3):
            group_wait(own, ring_s.at[direction, step])
        group_wait(own.at[pl.ds(0, SB // 2)], ring_s.at[direction, 3])
    for k in range(8):
        group_wait(stage.at[k, pl.ds(1, X - 1)], block_s.at[k])

    group_wait(lists_v.at[pl.ds(1, X - 1), 0:1], list_s)
    group_wait(gram_x.at[pl.ds(0, X - 1)], gx_s)
    group_wait(gram.at[pl.ds(0, Y - 1)], gg_s)
    for part in range(2):
        group_wait(recv_x.at[pl.ds(1, X - 1), cuts[part]], rx_s.at[part])

    group_wait(recv_y.at[pl.ds(1, Y - 1)], ry_r)
    mine = send_y[5].astype(F32)
    for e in range(1, Y):
        mine = mine + recv_y[e].astype(F32)
    group_wait(recv_y.at[pl.ds(1, Y - 1)], ry_s)
    out_ref[...] = jnp.dot(mine, inverse[...], precision=HIGHEST, preferred_element_type=F32)


def local(tiles, tile_blocks, counts, fetch_list, store_factor, day_factor):
    blocks = tile_blocks[0].T
    fetch = fetch_list.reshape(1, -1)
    store = store_factor.reshape(SB, TS, RANK)
    vmem = pl.BlockSpec(memory_space=pltpu.VMEM)
    hbm = pl.BlockSpec(memory_space=pl.ANY)
    bf16 = jnp.bfloat16
    dma = pltpu.SemaphoreType.DMA
    ring_buf = pltpu.VMEM((SB, TS, RANK), bf16)
    return pl.pallas_call(
        kernel,
        out_shape=jax.ShapeDtypeStruct((16, RANK), F32),
        in_specs=[hbm, hbm, pl.BlockSpec(memory_space=pltpu.SMEM), hbm, hbm, hbm],
        out_specs=vmem,
        scratch_shapes=[
            pltpu.VMEM(blocks.shape, jnp.int32), pltpu.VMEM(fetch.shape, jnp.int32), pltpu.VMEM(day_factor.shape, bf16),
            pltpu.VMEM(tiles.shape, bf16),
            ring_buf, ring_buf, ring_buf, ring_buf, ring_buf, ring_buf, ring_buf, ring_buf,
            pltpu.VMEM((Y, X, TS, RANK), bf16),
            pltpu.VMEM((Y, X, TS, RANK), bf16),
            pltpu.VMEM((X * Y, 64, RANK), F32),
            pltpu.VMEM((64, 64, RANK), F32),
            pltpu.VMEM((8, 128), jnp.int32),
            pltpu.SMEM((8, 128), jnp.int32),
            pltpu.VMEM((8, 128), jnp.int32),
            pltpu.VMEM((X, 8, 128), jnp.int32),
            pltpu.SMEM((X, 8, 128), jnp.int32),
            pltpu.VMEM((RANK, RANK), F32),
            pltpu.VMEM((X, 16, RANK), F32),
            pltpu.VMEM((16, RANK), F32),
            pltpu.VMEM((Y, 16, RANK), F32),
            pltpu.VMEM((RANK, RANK), F32),
            pltpu.VMEM((X, Y, 16, RANK), bf16),
            pltpu.VMEM((X, Y, 16, RANK), bf16),
            pltpu.VMEM((Y, 16, RANK), bf16),
            pltpu.VMEM((Y, 16, RANK), bf16),
            dma((8,)),
            dma((2, 4)), dma((2, 4, 4)),
            dma, dma,
            dma((8,)), dma((8,)),
            dma, dma, dma, dma,
            dma((2,)), dma((2,)), dma, dma,
        ],
        compiler_params=pltpu.CompilerParams(
            collective_id=0, has_side_effects=True, vmem_limit_bytes=60 * 1024 * 1024
        ),
    )(tiles, blocks, counts, fetch, store, day_factor)


def solution(mesh):
    return jax.shard_map(
        local,
        mesh=mesh,
        in_specs=(
            P(("prod", "store"), None, None),
            P(("prod", "store"), None, None),
            P(("prod", "store")),
            P(("prod", "store"), None, None),
            P("store", None),
            P(),
        ),
        out_specs=P(("prod", "store"), None),
        check_vma=False,
    )
```

```python
import jax
import jax.numpy as jnp
from jax import lax
from jax.experimental import pallas as pl
from jax.experimental.pallas import tpu as pltpu
from jax.sharding import PartitionSpec as P

PB = 16
SB = 8
TS = 64
RANK = 128
DAYS = 8
X = 8
Y = 8
HIGHEST = lax.Precision.HIGHEST
F32 = jnp.float32


def rows_sum(x):
    return jnp.sum(x, axis=0, keepdims=True)


def cols_sum(x):
    return jnp.sum(x, axis=1, keepdims=True)


def plan(blocks, count):
    slots = blocks.shape[1]
    sub = lax.broadcasted_iota(jnp.int32, (slots, slots), 0)
    lane = lax.broadcasted_iota(jnp.int32, (slots, slots), 1)
    lane_row = lax.broadcasted_iota(jnp.int32, (1, slots), 1)
    p_row, perm_row = blocks[0:1, :], blocks[1:2, :]
    key_row = jnp.where(lane_row < count, p_row * slots, PB * slots * 4) + perm_row
    eye = sub == lane
    perm_col = cols_sum(jnp.where(eye, perm_row, 0))
    key_col = cols_sum(jnp.where(eye, key_row, 0))
    rank_col = cols_sum(jnp.where(key_row < key_col, 1, 0))
    tile_of = rows_sum(jnp.where(perm_col == lane, sub, 0))
    order = rows_sum(jnp.where(rank_col == lane, perm_col, 0))
    block_at = rows_sum(jnp.where(rank_col == lane, key_col // slots, 0))
    block_before = rows_sum(jnp.where(rank_col + 1 == lane, key_col // slots, 0))
    same = jnp.where((block_at == block_before) & (lane_row > 0), 1, 0)
    ends = rows_sum(jnp.where(key_col < (lane + 1) * slots, 1, 0))
    begins = rows_sum(jnp.where(key_col < lane * slots, 1, 0))
    return tile_of, order, same, ends, begins


def kernel(
    tiles_hbm, blocks_hbm, count_ref, fetch_hbm, store_hbm, day_hbm, out_ref,
    blocks_ref, fetch_ref, day_ref, tiles, own, right1, right2, right3, left1, left2, left3, far,
    table, stage, contribs, sums,
    plan_v, plan_s, my_list, lists_v, lists_s,
    gram_part, gram_x, gram_sum, gram, inverse,
    send_x, recv_x, send_y, recv_y,
    local_sem, ring_s, ring_r, list_s, list_r, block_s, block_r,
    gx_s, gx_r, gg_s, gg_r, rx_s, rx_r, ry_s, ry_r,
):
    me = lax.axis_index("store")
    y, q = me // X, me % X

    def x_peer(d):
        return y * X + (q + d) % X

    def y_peer(e):
        return (y + e) % Y * X + q

    def to(src, dst, send, recv, target):
        return pltpu.make_async_remote_copy(
            src_ref=src, dst_ref=dst, send_sem=send, recv_sem=recv,
            device_id={"store": target}, device_id_type=pl.DeviceIdType.MESH,
        )

    def group_wait(ref, sem):
        pltpu.make_async_copy(ref, ref, sem).wait()

    def each(first, last, body, unroll=1):
        def step(i, carry):
            body(i)
            return carry
        lax.fori_loop(first, last, step, 0, unroll=unroll)

    barrier = pltpu.get_barrier_semaphore()

    def greet(target):
        pl.semaphore_signal(
            barrier, inc=1, device_id={"store": target}, device_id_type=pl.DeviceIdType.MESH)

    def load(src, dst, i):
        copy = pltpu.make_async_copy(src, dst, local_sem.at[i])
        copy.start()
        return copy

    greet(y_peer(1))
    greet(y_peer(Y - 1))
    each(1, X, lambda d: greet(x_peer(d)))
    load_fetch = load(fetch_hbm, fetch_ref, 0)
    load_own = load(store_hbm, own, 1)
    load_blocks = load(blocks_hbm, blocks_ref, 2)
    load_day = load(day_hbm, day_ref, 3)
    load_tiles = load(tiles_hbm, tiles, 4)
    load_fetch.wait()
    my_list[0:1, 0:64] = fetch_ref[...]
    load_own.wait()
    pl.semaphore_wait(barrier, X + 1)

    def list_copy(d):
        return to(
            my_list.at[0:1], lists_v.at[d, 0:1], list_s, list_r, x_peer(d)
        )

    each(1, X, lambda d: list_copy(d).start())

    rights, lefts = [right1, right2, right3, far], [left1, left2, left3, far]
    parts, size = 4, SB // 4

    def ring(direction, step, part):
        bufs = rights if direction == 0 else lefts
        src = own if step == 0 else bufs[step - 1]
        cut = pl.ds(part * size, size)
        return to(
            src.at[cut], bufs[step].at[cut],
            ring_s, ring_r.at[direction, step, part],
            y_peer(1 if direction == 0 else Y - 1),
        )

    for part in range(parts):
        ring(0, 0, part).start()
        ring(1, 0, part).start()

    def gram_add(*bufs):
        total = None
        for buf in bufs:
            rows = buf[...].reshape(SB * TS, RANK)
            part = lax.dot_general(
                rows, rows, (((0,), (0,)), ((), ())), preferred_element_type=F32
            )
            total = part if total is None else total + part
        return total

    load_blocks.wait()
    for row, value in enumerate(plan(blocks_ref[...], count_ref[0])):
        plan_v[row : row + 1, 0:64] = value
    load_plan = load(plan_v, plan_s, 5)
    lists_v[0, 0:1] = my_list[0:1]


    def block_copy(k, d):
        return to(stage.at[k, d], table.at[k, d], block_s, block_r.at[k], x_peer(d))

    def owner(k, d):
        shift = (0, Y - 1, 1, Y - 2, 2, Y - 3, 3, 4)[k]
        return (y + shift) % Y * X + (q + X - d) % X

    def serve(k, buf):
        mine = owner(k, 0)
        table[k, 0] = buf[lists_s[0, 0, mine] & (SB - 1)]

        def one(d):
            stage[k, d] = buf[lists_s[X - d, 0, mine] & (SB - 1)]
            block_copy(k, d).start()

        each(1, X, one)

    load_day.wait()
    day = day_ref[...].astype(F32)

    def contribute(k):
        def one(d):
            entry = owner(k, d)
            rows = table[k, d].astype(F32)
            kron = (rows[:, None, :] * day[None, :, :]).reshape(TS * DAYS, RANK).astype(jnp.bfloat16)
            contribs[entry] = jnp.dot(
                tiles[plan_s[0, entry] & 63], kron, preferred_element_type=F32
            )

        group_wait(table.at[k, pl.ds(1, X - 1)], block_r.at[k])
        each(0, X, one, unroll=4)

    def forward(step):
        for part in range(parts):
            for direction in range(2):
                ring(direction, step - 1, part).wait_recv()
                if step < 3 or part // 2 == direction:
                    ring(direction, step, part).start()

    lane8 = lax.broadcasted_iota(jnp.int32, (8, RANK), 1)
    sub8 = lax.broadcasted_iota(jnp.int32, (8, RANK), 0)
    lane_all = lax.broadcasted_iota(jnp.int32, (RANK, RANK), 1)
    sub_all = lax.broadcasted_iota(jnp.int32, (RANK, RANK), 0)

    def lane_of(rows, at):
        return jnp.broadcast_to(cols_sum(jnp.where(lane8 == at, rows, 0.0)), (8, RANK))

    def sub_of(rows, r):
        return jnp.broadcast_to(rows[r : r + 1, :], (8, RANK))

    def invert8(rows, first):
        columns = [lane_of(rows, first + r) for r in range(8)]
        d = {(i, j): sub_of(columns[j], i) for j in range(8) for i in range(j + 1)}
        for k in range(8):
            recip = 1.0 / d[k, k]
            row = [d[min(i, k), max(i, k)] for i in range(8)]
            scaled = [x * recip for x in row]
            for j in range(8):
                for i in range(j + 1):
                    if i != k and j != k:
                        d[i, j] = d[i, j] - scaled[i] * row[j]
            for i in range(8):
                if i != k:
                    d[min(i, k), max(i, k)] = scaled[i]
            d[k, k] = -recip
        out = []
        for r in range(8):
            column = -d[r, 7]
            for i in range(7):
                column = jnp.where(sub8 == i, -d[min(i, r), max(i, r)], column)
            out.append(column)
        return out

    def gj_apply(left, done_rows, first):
        change = lax.dot_general(
            left, done_rows, (((0,), (0,)), ((), ())), precision=HIGHEST, preferred_element_type=F32
        )
        inside = (lane_all >= first) & (lane_all < first + 8)
        rows_in = (sub_all >= first) & (sub_all < first + 8)
        new = jnp.where(inside, 0.0, inverse[...]) - change
        inverse[...] = jnp.where(rows_in, jnp.broadcast_to(done_rows[None], (16, 8, RANK)).reshape(RANK, RANK), new)

    def gj_start():
        zero = jnp.zeros((8, RANK), F32)
        return inverse[0:8, :], zero, zero

    def gj_step(b, state):
        rows, left, done_rows = state
        first = b * 8
        gj_apply(left, done_rows, first - 8)
        within = (lane8 >= first) & (lane8 < first + 8)
        columns = invert8(rows, first)
        unit = jnp.where(within, jnp.where(lane8 - first == sub8, 1.0, 0.0), rows)
        new = columns[0] * sub_of(unit, 0)
        for r in range(1, 8):
            new = new + columns[r] * sub_of(unit, r)
        new_left = jnp.where(within, 0.0, jnp.where(lane8 < first, -rows, rows))
        after = inverse[pl.ds(pl.multiple_of(jnp.minimum(first + 8, RANK - 8), 8), 8), :]
        step = lane_of(after, first) * sub_of(new, 0)
        for r in range(1, 8):
            step = step + lane_of(after, first + r) * sub_of(new, r)
        return jnp.where(within, 0.0, after) - step, new_left, new

    def gj_end(state):
        gj_apply(state[1], state[2], RANK - 8)

    gram_part[...] = gram_add(own)
    forward(1)
    group_wait(lists_v.at[pl.ds(1, X - 1), 0:1], list_r)
    load(lists_v, lists_s, 6).wait()
    serve(0, own)
    serve(1, right1)
    serve(2, left1)
    gram_part[...] += gram_add(right1, left1)
    forward(2)
    serve(3, right2)
    serve(4, left2)
    gram_part[...] += gram_add(right2, left2)
    forward(3)
    serve(5, right3)
    serve(6, left3)
    gram_part[...] += gram_add(right3, left3)
    for part in range(2):
        ring(0, 3, part).wait_recv()
        ring(1, 3, 2 + part).wait_recv()
    serve(7, far)
    gram_part[...] += gram_add(far)

    gram_x[q] = gram_part[pl.ds(y * 16, 16), :]

    def gram_x_copy(d):
        return to(
            gram_part.at[pl.ds(y * 16, 16)], gram_x.at[q], gx_s, gx_r, x_peer(d)
        )

    def gram_g_copy(e):
        return to(gram_sum, gram.at[y], gg_s, gg_r, y_peer(e))

    each(1, X, lambda d: gram_x_copy(d).start())
    load_tiles.wait()
    load_plan.wait()
    for k in range(5):
        contribute(k)
    group_wait(gram_x.at[pl.ds(0, X - 1)], gx_r)
    total = gram_x[0]
    for i in range(1, X):
        total = total + gram_x[i]
    gram_sum[...] = total
    gram[y] = total
    each(1, Y, lambda e: gram_g_copy(e).start())
    contribute(5)
    contribute(6)
    contribute(7)

    def add(r, run):
        run = contribs[plan_s[1, r] & 63] + jnp.where(plan_s[2, r] == 1, run, 0.0)
        sums[r] = run
        return run

    lax.fori_loop(0, 64, add, jnp.zeros((TS, RANK), F32), unroll=8)

    def pick(place):
        i = (y + place + 3) % Y
        for j in range(2):
            p = 2 * i + j
            end = plan_s[3, p]
            value = sums[jnp.maximum(end - 1, 0) & 63]
            value = jnp.where(end > plan_s[4, p], value, 0.0).astype(jnp.bfloat16)
            for part in range(4):
                send_x[4 * j + part, place] = value[16 * part : 16 * part + 16]


    cuts = (pl.ds(0, 3), pl.ds(3, 5))

    def rx_copy(d, part):
        return to(
            send_x.at[(q + d) % X, cuts[part]], recv_x.at[d, cuts[part]],
            rx_s.at[part], rx_r.at[part], x_peer(d),
        )

    def ry_copy(e):
        return to(send_y.at[(e + 5) % Y], recv_y.at[e], ry_s, ry_r, y_peer(e))

    def sum_x(part):
        group_wait(recv_x.at[pl.ds(1, X - 1), cuts[part]], rx_r.at[part])
        share = send_x[q, cuts[part]].astype(F32)
        for d in range(1, X):
            share = share + recv_x[d, cuts[part]].astype(F32)
        send_y[cuts[part]] = share.astype(jnp.bfloat16)

    each(0, 3, pick, unroll=3)
    each(1, X, lambda d: rx_copy(d, 0).start())
    each(3, 8, pick, unroll=5)
    each(1, X, lambda d: rx_copy(d, 1).start())
    group_wait(gram.at[pl.ds(0, Y - 1)], gg_r)
    gram_day = lax.dot_general(
        day_ref[...], day_ref[...], (((0,), (0,)), ((), ())), preferred_element_type=F32
    )
    inverse[...] = gram[...].reshape(RANK, RANK) * gram_day
    state = lax.fori_loop(0, 6, gj_step, gj_start())
    sum_x(0)
    each(3, 6, lambda e: ry_copy(e).start())
    state = lax.fori_loop(6, 8, gj_step, state)
    sum_x(1)
    each(1, 3, lambda e: ry_copy(e).start())
    each(6, 8, lambda e: ry_copy(e).start())
    gj_end(lax.fori_loop(8, 16, gj_step, state))

    group_wait(stage.at[pl.ds(0, 8), pl.ds(1, X - 1)], ring_s)
    group_wait(stage.at[pl.ds(0, 8), pl.ds(1, X - 1)], block_s)

    group_wait(lists_v.at[pl.ds(1, X - 1), 0:1], list_s)
    group_wait(gram_x.at[pl.ds(0, X - 1)], gx_s)
    group_wait(gram.at[pl.ds(0, Y - 1)], gg_s)
    for part in range(2):
        group_wait(recv_x.at[pl.ds(1, X - 1), cuts[part]], rx_s.at[part])

    group_wait(recv_y.at[pl.ds(1, Y - 1)], ry_r)
    mine = send_y[5].astype(F32)
    for e in range(1, Y):
        mine = mine + recv_y[e].astype(F32)
    group_wait(recv_y.at[pl.ds(1, Y - 1)], ry_s)
    out_ref[...] = jnp.dot(mine, inverse[...], precision=HIGHEST, preferred_element_type=F32)


def local(tiles, tile_blocks, counts, fetch_list, store_factor, day_factor):
    blocks = tile_blocks[0].T
    fetch = fetch_list.reshape(1, -1)
    store = store_factor.reshape(SB, TS, RANK)
    vmem = pl.BlockSpec(memory_space=pltpu.VMEM)
    hbm = pl.BlockSpec(memory_space=pl.ANY)
    bf16 = jnp.bfloat16
    dma = pltpu.SemaphoreType.DMA
    ring_buf = pltpu.VMEM((SB, TS, RANK), bf16)
    return pl.pallas_call(
        kernel,
        out_shape=jax.ShapeDtypeStruct((16, RANK), F32),
        in_specs=[hbm, hbm, pl.BlockSpec(memory_space=pltpu.SMEM), hbm, hbm, hbm],
        out_specs=vmem,
        scratch_shapes=[
            pltpu.VMEM(blocks.shape, jnp.int32), pltpu.VMEM(fetch.shape, jnp.int32), pltpu.VMEM(day_factor.shape, bf16),
            pltpu.VMEM(tiles.shape, bf16),
            ring_buf, ring_buf, ring_buf, ring_buf, ring_buf, ring_buf, ring_buf, ring_buf,
            pltpu.VMEM((Y, X, TS, RANK), bf16),
            pltpu.VMEM((Y, X, TS, RANK), bf16),
            pltpu.VMEM((X * Y, 64, RANK), F32),
            pltpu.VMEM((64, 64, RANK), F32),
            pltpu.VMEM((8, 128), jnp.int32),
            pltpu.SMEM((8, 128), jnp.int32),
            pltpu.VMEM((8, 128), jnp.int32),
            pltpu.VMEM((X, 8, 128), jnp.int32),
            pltpu.SMEM((X, 8, 128), jnp.int32),
            pltpu.VMEM((RANK, RANK), F32),
            pltpu.VMEM((X, 16, RANK), F32),
            pltpu.VMEM((16, RANK), F32),
            pltpu.VMEM((Y, 16, RANK), F32),
            pltpu.VMEM((RANK, RANK), F32),
            pltpu.VMEM((X, Y, 16, RANK), bf16),
            pltpu.VMEM((X, Y, 16, RANK), bf16),
            pltpu.VMEM((Y, 16, RANK), bf16),
            pltpu.VMEM((Y, 16, RANK), bf16),
            dma((8,)),
            dma, dma((2, 4, 4)),
            dma, dma,
            dma, dma((8,)),
            dma, dma, dma, dma,
            dma((2,)), dma((2,)), dma, dma,
        ],
        compiler_params=pltpu.CompilerParams(
            collective_id=0, has_side_effects=True, vmem_limit_bytes=60 * 1024 * 1024
        ),
    )(tiles, blocks, counts, fetch, store, day_factor)


def solution(mesh):
    return jax.shard_map(
        local,
        mesh=mesh,
        in_specs=(
            P(("prod", "store"), None, None),
            P(("prod", "store"), None, None),
            P(("prod", "store")),
            P(("prod", "store"), None, None),
            P("store", None),
            P(),
        ),
        out_specs=P(("prod", "store"), None),
        check_vma=False,
    )
```

```python
import jax
import jax.numpy as jnp
from jax import lax
from jax.experimental import pallas as pl
from jax.experimental.pallas import tpu as pltpu
from jax.sharding import PartitionSpec as P

PB = 16
SB = 8
TS = 64
RANK = 128
DAYS = 8
X = 8
Y = 8
HIGHEST = lax.Precision.HIGHEST
F32 = jnp.float32


def rows_sum(x):
    return jnp.sum(x, axis=0, keepdims=True)


def cols_sum(x):
    return jnp.sum(x, axis=1, keepdims=True)


def plan(blocks, count):
    slots = blocks.shape[1]
    sub = lax.broadcasted_iota(jnp.int32, (slots, slots), 0)
    lane = lax.broadcasted_iota(jnp.int32, (slots, slots), 1)
    lane_row = lax.broadcasted_iota(jnp.int32, (1, slots), 1)
    p_row, perm_row = blocks[0:1, :], blocks[1:2, :]
    key_row = jnp.where(lane_row < count, p_row * slots, PB * slots * 4) + perm_row
    eye = sub == lane
    perm_col = cols_sum(jnp.where(eye, perm_row, 0))
    key_col = cols_sum(jnp.where(eye, key_row, 0))
    rank_col = cols_sum(jnp.where(key_row < key_col, 1, 0))
    tile_of = rows_sum(jnp.where(perm_col == lane, sub, 0))
    order = rows_sum(jnp.where(rank_col == lane, perm_col, 0))
    block_at = rows_sum(jnp.where(rank_col == lane, key_col // slots, 0))
    block_before = rows_sum(jnp.where(rank_col + 1 == lane, key_col // slots, 0))
    same = jnp.where((block_at == block_before) & (lane_row > 0), 1, 0)
    ends = rows_sum(jnp.where(key_col < (lane + 1) * slots, 1, 0))
    begins = rows_sum(jnp.where(key_col < lane * slots, 1, 0))
    return tile_of, order, same, ends, begins


def kernel(
    tiles_hbm, blocks_hbm, count_ref, fetch_hbm, store_hbm, day_hbm, out_ref,
    blocks_ref, fetch_ref, day_ref, tiles, own, right1, right2, right3, left1, left2, left3, far,
    table, stage, contribs, sums,
    plan_v, plan_s, my_list, lists_v, lists_s,
    gram_part, gram_x, gram_sum, gram, inverse,
    send_x, recv_x, send_y, recv_y,
    local_sem, ring_s, ring_r, list_s, list_r, block_s, block_r,
    gx_s, gx_r, gg_s, gg_r, rx_s, rx_r, ry_s, ry_r,
):
    me = lax.axis_index("store")
    y, q = me // X, me % X

    def x_peer(d):
        return y * X + (q + d) % X

    def y_peer(e):
        return (y + e) % Y * X + q

    def to(src, dst, send, recv, target):
        return pltpu.make_async_remote_copy(
            src_ref=src, dst_ref=dst, send_sem=send, recv_sem=recv,
            device_id={"store": target}, device_id_type=pl.DeviceIdType.MESH,
        )

    def group_wait(ref, sem):
        pltpu.make_async_copy(ref, ref, sem).wait()

    def each(first, last, body, unroll=1):
        def step(i, carry):
            body(i)
            return carry
        lax.fori_loop(first, last, step, 0, unroll=unroll)

    barrier = pltpu.get_barrier_semaphore()

    def greet(target):
        pl.semaphore_signal(
            barrier, inc=1, device_id={"store": target}, device_id_type=pl.DeviceIdType.MESH)

    def load(src, dst, i):
        copy = pltpu.make_async_copy(src, dst, local_sem.at[i])
        copy.start()
        return copy

    greet(y_peer(1))
    greet(y_peer(Y - 1))
    each(1, X, lambda d: greet(x_peer(d)))
    load_fetch = load(fetch_hbm, fetch_ref, 0)
    load_own = load(store_hbm, own, 1)
    load_blocks = load(blocks_hbm, blocks_ref, 2)
    load_day = load(day_hbm, day_ref, 3)
    load_tiles = load(tiles_hbm, tiles, 4)
    load_fetch.wait()
    my_list[0:1, 0:64] = fetch_ref[...]
    load_own.wait()
    pl.semaphore_wait(barrier, X + 1)

    def list_copy(d):
        return to(
            my_list.at[0:1], lists_v.at[d, 0:1], list_s, list_r, x_peer(d)
        )

    each(1, X, lambda d: list_copy(d).start())

    rights, lefts = [right1, right2, right3, far], [left1, left2, left3, far]
    parts, size = 4, SB // 4

    def ring(direction, step, part):
        bufs = rights if direction == 0 else lefts
        src = own if step == 0 else bufs[step - 1]
        cut = pl.ds(part * size, size)
        return to(
            src.at[cut], bufs[step].at[cut],
            ring_s, ring_r.at[direction, step, part],
            y_peer(1 if direction == 0 else Y - 1),
        )

    for part in range(parts):
        ring(0, 0, part).start()
        ring(1, 0, part).start()

    def gram_add(*bufs):
        total = None
        for buf in bufs:
            rows = buf[...].reshape(SB * TS, RANK)
            part = lax.dot_general(
                rows, rows, (((0,), (0,)), ((), ())), preferred_element_type=F32
            )
            total = part if total is None else total + part
        return total

    load_blocks.wait()
    for row, value in enumerate(plan(blocks_ref[...], count_ref[0])):
        plan_v[row : row + 1, 0:64] = value
    load_plan = load(plan_v, plan_s, 5)
    lists_v[0, 0:1] = my_list[0:1]


    def block_copy(k, d):
        return to(stage.at[k, d], table.at[k, d], block_s, block_r.at[k], x_peer(d))

    def owner(k, d):
        shift = (0, Y - 1, 1, Y - 2, 2, Y - 3, 3, 4)[k]
        return (y + shift) % Y * X + (q + X - d) % X

    def serve(k, buf):
        mine = owner(k, 0)
        table[k, 0] = buf[lists_s[0, 0, mine] & (SB - 1)]

        def one(d):
            stage[k, d] = buf[lists_s[X - d, 0, mine] & (SB - 1)]
            block_copy(k, d).start()

        each(1, X, one)

    load_day.wait()
    day = day_ref[...].astype(F32)

    def contribute(k):
        def one(d):
            entry = owner(k, d)
            rows = table[k, d].astype(F32)
            kron = (rows[:, None, :] * day[None, :, :]).reshape(TS * DAYS, RANK).astype(jnp.bfloat16)
            contribs[entry] = jnp.dot(
                tiles[plan_s[0, entry] & 63], kron, preferred_element_type=F32
            )

        group_wait(table.at[k, pl.ds(1, X - 1)], block_r.at[k])
        each(0, X, one, unroll=4)

    def forward(step, first=0, last=parts):
        for part in range(first, last):
            for direction in range(2):
                ring(direction, step - 1, part).wait_recv()
                if step < 3 or part // 2 == direction:
                    ring(direction, step, part).start()

    lane8 = lax.broadcasted_iota(jnp.int32, (8, RANK), 1)
    sub8 = lax.broadcasted_iota(jnp.int32, (8, RANK), 0)
    lane_all = lax.broadcasted_iota(jnp.int32, (RANK, RANK), 1)
    sub_all = lax.broadcasted_iota(jnp.int32, (RANK, RANK), 0)

    def lane_of(rows, at):
        return jnp.broadcast_to(cols_sum(jnp.where(lane8 == at, rows, 0.0)), (8, RANK))

    def sub_of(rows, r):
        return jnp.broadcast_to(rows[r : r + 1, :], (8, RANK))

    def invert8(rows, first):
        columns = [lane_of(rows, first + r) for r in range(8)]
        d = {(i, j): sub_of(columns[j], i) for j in range(8) for i in range(j + 1)}
        for k in range(8):
            recip = 1.0 / d[k, k]
            row = [d[min(i, k), max(i, k)] for i in range(8)]
            scaled = [x * recip for x in row]
            for j in range(8):
                for i in range(j + 1):
                    if i != k and j != k:
                        d[i, j] = d[i, j] - scaled[i] * row[j]
            for i in range(8):
                if i != k:
                    d[min(i, k), max(i, k)] = scaled[i]
            d[k, k] = -recip
        out = []
        for r in range(8):
            column = -d[r, 7]
            for i in range(7):
                column = jnp.where(sub8 == i, -d[min(i, r), max(i, r)], column)
            out.append(column)
        return out

    def gj_apply(left, done_rows, first):
        change = lax.dot_general(
            left, done_rows, (((0,), (0,)), ((), ())), precision=HIGHEST, preferred_element_type=F32
        )
        inside = (lane_all >= first) & (lane_all < first + 8)
        rows_in = (sub_all >= first) & (sub_all < first + 8)
        new = jnp.where(inside, 0.0, inverse[...]) - change
        inverse[...] = jnp.where(rows_in, jnp.broadcast_to(done_rows[None], (16, 8, RANK)).reshape(RANK, RANK), new)

    def gj_start():
        zero = jnp.zeros((8, RANK), F32)
        return inverse[0:8, :], zero, zero

    def gj_step(b, state):
        rows, left, done_rows = state
        first = b * 8
        gj_apply(left, done_rows, first - 8)
        within = (lane8 >= first) & (lane8 < first + 8)
        columns = invert8(rows, first)
        unit = jnp.where(within, jnp.where(lane8 - first == sub8, 1.0, 0.0), rows)
        new = columns[0] * sub_of(unit, 0)
        for r in range(1, 8):
            new = new + columns[r] * sub_of(unit, r)
        new_left = jnp.where(within, 0.0, jnp.where(lane8 < first, -rows, rows))
        after = inverse[pl.ds(pl.multiple_of(jnp.minimum(first + 8, RANK - 8), 8), 8), :]
        step = lane_of(after, first) * sub_of(new, 0)
        for r in range(1, 8):
            step = step + lane_of(after, first + r) * sub_of(new, r)
        return jnp.where(within, 0.0, after) - step, new_left, new

    def gj_end(state):
        gj_apply(state[1], state[2], RANK - 8)

    gram_part[...] = gram_add(own)
    forward(1, 0, 2)
    group_wait(lists_v.at[pl.ds(1, X - 1), 0:1], list_r)
    load_lists = load(lists_v, lists_s, 6)
    forward(1, 2)
    load_lists.wait()
    serve(0, own)
    serve(1, right1)
    serve(2, left1)
    gram_part[...] += gram_add(right1, left1)
    forward(2)
    serve(3, right2)
    serve(4, left2)
    gram_part[...] += gram_add(right2, left2)
    forward(3)
    serve(5, right3)
    serve(6, left3)
    gram_part[...] += gram_add(right3, left3)
    for part in range(2):
        ring(0, 3, part).wait_recv()
        ring(1, 3, 2 + part).wait_recv()
    serve(7, far)
    gram_part[...] += gram_add(far)

    gram_x[q] = gram_part[pl.ds(y * 16, 16), :]

    def gram_x_copy(d):
        return to(
            gram_part.at[pl.ds(y * 16, 16)], gram_x.at[q], gx_s, gx_r, x_peer(d)
        )

    def gram_g_copy(e):
        return to(gram_sum, gram.at[y], gg_s, gg_r, y_peer(e))

    each(1, X, lambda d: gram_x_copy(d).start())
    load_tiles.wait()
    load_plan.wait()
    for k in range(5):
        contribute(k)
    group_wait(gram_x.at[pl.ds(0, X - 1)], gx_r)
    total = gram_x[0]
    for i in range(1, X):
        total = total + gram_x[i]
    gram_sum[...] = total
    gram[y] = total
    each(1, Y, lambda e: gram_g_copy(e).start())
    contribute(5)
    contribute(6)
    contribute(7)

    def add(r, run):
        run = contribs[plan_s[1, r] & 63] + jnp.where(plan_s[2, r] == 1, run, 0.0)
        sums[r] = run
        return run

    lax.fori_loop(0, 64, add, jnp.zeros((TS, RANK), F32), unroll=8)

    def pick(place):
        i = (y + place + 3) % Y
        for j in range(2):
            p = 2 * i + j
            end = plan_s[3, p]
            value = sums[jnp.maximum(end - 1, 0) & 63]
            value = jnp.where(end > plan_s[4, p], value, 0.0).astype(jnp.bfloat16)
            for part in range(4):
                send_x[4 * j + part, place] = value[16 * part : 16 * part + 16]


    cuts = (pl.ds(0, 3), pl.ds(3, 5))

    def rx_copy(d, part):
        return to(
            send_x.at[(q + d) % X, cuts[part]], recv_x.at[d, cuts[part]],
            rx_s.at[part], rx_r.at[part], x_peer(d),
        )

    def ry_copy(e):
        return to(send_y.at[(e + 5) % Y], recv_y.at[e], ry_s, ry_r, y_peer(e))

    def sum_x(part):
        group_wait(recv_x.at[pl.ds(1, X - 1), cuts[part]], rx_r.at[part])
        share = send_x[q, cuts[part]].astype(F32)
        for d in range(1, X):
            share = share + recv_x[d, cuts[part]].astype(F32)
        send_y[cuts[part]] = share.astype(jnp.bfloat16)

    each(0, 3, pick, unroll=3)
    each(1, X, lambda d: rx_copy(d, 0).start())
    each(3, 8, pick, unroll=5)
    each(1, X, lambda d: rx_copy(d, 1).start())
    group_wait(gram.at[pl.ds(0, Y - 1)], gg_r)
    gram_day = lax.dot_general(
        day_ref[...], day_ref[...], (((0,), (0,)), ((), ())), preferred_element_type=F32
    )
    inverse[...] = gram[...].reshape(RANK, RANK) * gram_day
    state = lax.fori_loop(0, 6, gj_step, gj_start())
    sum_x(0)
    each(3, 6, lambda e: ry_copy(e).start())
    state = lax.fori_loop(6, 8, gj_step, state)
    sum_x(1)
    each(1, 3, lambda e: ry_copy(e).start())
    each(6, 8, lambda e: ry_copy(e).start())
    gj_end(lax.fori_loop(8, 16, gj_step, state))

    group_wait(stage.at[pl.ds(0, 8), pl.ds(1, X - 1)], ring_s)
    group_wait(stage.at[pl.ds(0, 8), pl.ds(1, X - 1)], block_s)

    group_wait(lists_v.at[pl.ds(1, X - 1), 0:1], list_s)
    group_wait(gram_x.at[pl.ds(0, X - 1)], gx_s)
    group_wait(gram.at[pl.ds(0, Y - 1)], gg_s)
    for part in range(2):
        group_wait(recv_x.at[pl.ds(1, X - 1), cuts[part]], rx_s.at[part])

    group_wait(recv_y.at[pl.ds(1, Y - 1)], ry_r)
    mine = send_y[5].astype(F32)
    for e in range(1, Y):
        mine = mine + recv_y[e].astype(F32)
    group_wait(recv_y.at[pl.ds(1, Y - 1)], ry_s)
    out_ref[...] = jnp.dot(mine, inverse[...], precision=HIGHEST, preferred_element_type=F32)


def local(tiles, tile_blocks, counts, fetch_list, store_factor, day_factor):
    blocks = tile_blocks[0].T
    fetch = fetch_list.reshape(1, -1)
    store = store_factor.reshape(SB, TS, RANK)
    vmem = pl.BlockSpec(memory_space=pltpu.VMEM)
    hbm = pl.BlockSpec(memory_space=pl.ANY)
    bf16 = jnp.bfloat16
    dma = pltpu.SemaphoreType.DMA
    ring_buf = pltpu.VMEM((SB, TS, RANK), bf16)
    return pl.pallas_call(
        kernel,
        out_shape=jax.ShapeDtypeStruct((16, RANK), F32),
        in_specs=[hbm, hbm, pl.BlockSpec(memory_space=pltpu.SMEM), hbm, hbm, hbm],
        out_specs=vmem,
        scratch_shapes=[
            pltpu.VMEM(blocks.shape, jnp.int32), pltpu.VMEM(fetch.shape, jnp.int32), pltpu.VMEM(day_factor.shape, bf16),
            pltpu.VMEM(tiles.shape, bf16),
            ring_buf, ring_buf, ring_buf, ring_buf, ring_buf, ring_buf, ring_buf, ring_buf,
            pltpu.VMEM((Y, X, TS, RANK), bf16),
            pltpu.VMEM((Y, X, TS, RANK), bf16),
            pltpu.VMEM((X * Y, 64, RANK), F32),
            pltpu.VMEM((64, 64, RANK), F32),
            pltpu.VMEM((8, 128), jnp.int32),
            pltpu.SMEM((8, 128), jnp.int32),
            pltpu.VMEM((8, 128), jnp.int32),
            pltpu.VMEM((X, 8, 128), jnp.int32),
            pltpu.SMEM((X, 8, 128), jnp.int32),
            pltpu.VMEM((RANK, RANK), F32),
            pltpu.VMEM((X, 16, RANK), F32),
            pltpu.VMEM((16, RANK), F32),
            pltpu.VMEM((Y, 16, RANK), F32),
            pltpu.VMEM((RANK, RANK), F32),
            pltpu.VMEM((X, Y, 16, RANK), bf16),
            pltpu.VMEM((X, Y, 16, RANK), bf16),
            pltpu.VMEM((Y, 16, RANK), bf16),
            pltpu.VMEM((Y, 16, RANK), bf16),
            dma((8,)),
            dma, dma((2, 4, 4)),
            dma, dma,
            dma, dma((8,)),
            dma, dma, dma, dma,
            dma((2,)), dma((2,)), dma, dma,
        ],
        compiler_params=pltpu.CompilerParams(
            collective_id=0, has_side_effects=True, vmem_limit_bytes=60 * 1024 * 1024
        ),
    )(tiles, blocks, counts, fetch, store, day_factor)


def solution(mesh):
    return jax.shard_map(
        local,
        mesh=mesh,
        in_specs=(
            P(("prod", "store"), None, None),
            P(("prod", "store"), None, None),
            P(("prod", "store")),
            P(("prod", "store"), None, None),
            P("store", None),
            P(),
        ),
        out_specs=P(("prod", "store"), None),
        check_vma=False,
    )
```
